512 devices in a mesh: dp: 128 (over y_lo, x, z, core), tensor: 4 (over y_hi).
Axes of the slice: x: 4, y: 8 (y_hi: 4, y_lo: 2; y = y_hi * 2 + y_lo), z: 8, core: 2. Of those that a mesh axis runs over, the one named last changes fastest.
Arguments:
- image_pooled: bfloat16 [8192, 1152], P('dp'), may hold values from -64 to 64
- text_pooled: bfloat16 [8192, 1152], P('dp'), may hold values from -64 to 64
- image_norm_gain: float32 [1152], replicated, may hold values from 0.5 to 1.5
- image_norm_bias: float32 [1152], replicated, may hold values from -3 to 3
- image_up: bfloat16 [1152, 4304], P('dp', 'tensor'), may hold values from -0.1875 to 0.1875
- image_up_bias: float32 [4304], P('tensor'), may hold values from -3 to 3
- image_down: bfloat16 [4304, 1152], P('tensor', 'dp'), may hold values from -0.09375 to 0.09375
- image_down_bias: float32 [1152], replicated, may hold values from -2 to 2
- text_norm_gain: float32 [1152], replicated, may hold values from 0.5 to 1.5
- text_norm_bias: float32 [1152], replicated, may hold values from -2 to 2
- text_head: bfloat16 [1152, 1152], P('tensor'), may hold values from -0.25 to 1.25
- text_head_bias: float32 [1152], replicated, may hold values from -2 to 2
- log_scale: float32 [1], replicated, may hold values from 3.7 to 4.8
- logit_shift: float32 [1], replicated, may hold values from -14 to -8
- loss_scale: float32 [1], replicated, may hold values from 128 to 1024
Outputs:
- image_grad: float32 [8192, 1152], P('dp')
- text_grad: float32 [8192, 1152], P('dp')
The draws below stay inside these ranges and needn't reach their ends.
All inputs are finite; a program needn't handle non-finite values.
Results may differ from the reference program's by a relative error of at most 0.019.
Values may be sent and summed in bfloat16 or wider, within the bound.
No kernel may reach another device: no remote copies, remote signals or barrier semaphores. Data moves between devices by JAX's collectives and lax.ppermute only.
A program may use at most 64 MiB of HBM per device.

```python
import math
import jax
import jax.numpy as jnp
from jax import lax

D = 1152
FF = 4304
PAIRS = 8192


def shared_latent(key):
    return jax.random.normal(key, (PAIRS, D), jnp.float32)


def draw_image_pooled(key, part):
    common = shared_latent(key)
    key = jax.random.fold_in(key, 11)
    noise_key = jax.random.fold_in(key, 0)
    noise = jax.random.normal(noise_key, (PAIRS, D), jnp.float32)
    return (0.6 * common + 0.8 * noise).astype(jnp.bfloat16)


def draw_text_pooled(key, part):
    common = shared_latent(key)
    key = jax.random.fold_in(key, 13)
    noise_key = jax.random.fold_in(key, 0)
    noise = jax.random.normal(noise_key, (PAIRS, D), jnp.float32)
    return (0.6 * common + 0.8 * noise).astype(jnp.bfloat16)


def draw_text_head(key, part):
    key = jax.random.fold_in(key, 23)
    noise = jax.random.truncated_normal(key, -3.0, 3.0, (D, D), jnp.float32) * (0.7 / math.sqrt(D))
    return (jnp.eye(D, dtype=jnp.float32) + noise).astype(jnp.bfloat16)


def level_of(own_key, dims, cuts, least, high):
    level = 1.0
    for axis_at, parts in cuts:
        heights = jax.random.uniform(jax.random.fold_in(jax.random.fold_in(own_key, 6), axis_at), (parts,), jnp.float32, least / len(cuts), high / len(cuts))
        level = level * jnp.repeat(jnp.exp(heights), dims[axis_at] // parts).reshape((-1,) + (1,) * (len(dims) - 1 - axis_at))
    return level


def bell_draw(own_key, extent, spread, most, pieces=(), held_as=jnp.bfloat16):
    entries = spread * jax.random.normal(own_key, extent, jnp.float32)
    if pieces:
        entries = entries * level_of(own_key, extent, pieces, -0.22, 0.18)
    return jnp.clip(entries, -most, most).astype(held_as)


def setup_inputs(seed: int = 0) -> dict:
    keys = jax.random.split(jax.random.key(seed), 16)
    return {
        "image_pooled": draw_image_pooled(jax.random.fold_in(keys[15], 71), 0),
        "text_pooled": draw_text_pooled(jax.random.fold_in(keys[15], 71), 0),
        "image_norm_gain": jnp.clip(1.0 + 0.1 * jax.random.normal(keys[2], (D,), jnp.float32), 0.5, 1.5),
        "image_norm_bias": bell_draw(keys[3], (D,), 0.5, 3.0, (), jnp.float32),
        "image_up": bell_draw(keys[4], (D, FF), D ** -0.5, 0.1875, ((0, 128), (1, 4))),
        "image_up_bias": bell_draw(keys[5], (FF,), 0.5, 3.0, ((0, 4),), jnp.float32),
        "image_down": bell_draw(keys[6], (FF, D), FF ** -0.5, 0.09375, ((0, 4), (1, 128))),
        "image_down_bias": bell_draw(keys[7], (D,), 0.3, 2.0, (), jnp.float32),
        "text_norm_gain": jnp.clip(1.0 + 0.1 * jax.random.normal(keys[8], (D,), jnp.float32), 0.5, 1.5),
        "text_norm_bias": bell_draw(keys[9], (D,), 0.3, 2.0, (), jnp.float32),
        "text_head": draw_text_head(jax.random.fold_in(keys[15], 71), 0),
        "text_head_bias": bell_draw(keys[11], (D,), 0.3, 2.0, (), jnp.float32),
        "log_scale": jnp.clip(jax.random.uniform(keys[12], (1,), jnp.float32, 3.7, 4.8), 3.7, 4.8),
        "logit_shift": jnp.clip(jax.random.uniform(keys[13], (1,), jnp.float32, -14.0, -8.0), -14.0, -8.0),
        "loss_scale": jnp.clip(jnp.exp(jax.random.uniform(keys[14], (1,), jnp.float32, math.log(128.0), math.log(1024.0))), 128.0, 1024.0),
    }


epsilon = 1e-06
tanh_coef = 0.7978845608028654
cubic_coef = 0.044715

def gelu_parts(preact):
    inside = tanh_coef * (preact + cubic_coef * preact * preact * preact)
    tangent = jnp.tanh(inside)
    activated = 0.5 * preact * (1.0 + tangent)
    derivative = 0.5 * (1.0 + tangent) + 0.5 * preact * (1.0 - tangent * tangent) * tanh_coef * (1.0 + 3.0 * cubic_coef * preact * preact)
    return (activated, derivative)

def norm_forward(source, gain_vec, bias_vec):
    centre = source - lax.optimization_barrier(jnp.mean(source, axis=1, keepdims=True))
    inverse = lax.rsqrt(lax.optimization_barrier(jnp.mean(centre * centre, axis=1, keepdims=True)) + epsilon)
    normed = centre * inverse
    return (normed * gain_vec + bias_vec, normed, inverse)

def norm_backward(upstream, normed, inverse, gain_vec):
    scaled = upstream * gain_vec
    return inverse * (scaled - lax.optimization_barrier(jnp.mean(scaled, axis=1, keepdims=True)) - normed * lax.optimization_barrier(jnp.mean(scaled * normed, axis=1, keepdims=True)))

def unit_length(summed):
    inverse = lax.rsqrt(lax.optimization_barrier(jnp.sum(summed * summed, axis=1, keepdims=True)) + epsilon)
    return (summed * inverse, inverse)

def reference(image_pooled, text_pooled, image_norm_gain, image_norm_bias, image_up, image_up_bias, image_down, image_down_bias, text_norm_gain, text_norm_bias, text_head, text_head_bias, log_scale, logit_shift, loss_scale):
    image_float = image_pooled.astype(jnp.float32)
    image_ready, image_normed, image_inverse = norm_forward(image_float, image_norm_gain, image_norm_bias)
    hidden_pre = jnp.dot(image_ready.astype(jnp.bfloat16), image_up, preferred_element_type=jnp.float32) + image_up_bias
    hidden_act, hidden_slope = gelu_parts(hidden_pre)
    image_sum = image_float + jnp.dot(hidden_act.astype(jnp.bfloat16), image_down, preferred_element_type=jnp.float32) + image_down_bias
    image_unit, image_invnorm = unit_length(image_sum)
    text_float = text_pooled.astype(jnp.float32)
    text_ready, text_normed, text_inverse = norm_forward(text_float, text_norm_gain, text_norm_bias)
    text_sum = jnp.dot(text_ready.astype(jnp.bfloat16), text_head, preferred_element_type=jnp.float32) + text_head_bias
    text_unit, text_invnorm = unit_length(text_sum)
    image_emb = image_unit.astype(jnp.bfloat16)
    text_emb = text_unit.astype(jnp.bfloat16)
    scale_value = jnp.exp(log_scale[0])
    factor = loss_scale[0] * scale_value / PAIRS
    block_rows = math.gcd(PAIRS, 512)
    block_count = PAIRS // block_rows
    text_ids = jnp.arange(PAIRS, dtype=jnp.int32)

    def block_step(text_carry, block_index):
        first_row = (block_index * block_rows).astype(jnp.int32)
        image_block = lax.dynamic_slice_in_dim(image_emb, first_row, block_rows, 0)
        scores = lax.dot_general(image_block, text_emb, (((1,), (1,)), ((), ())), preferred_element_type=jnp.float32)
        image_ids = first_row + jnp.arange(block_rows, dtype=jnp.int32)
        diagonal = (image_ids[:, None] == text_ids[None, :]).astype(jnp.float32)
        pair_coef = (factor * (jax.nn.sigmoid(scale_value * scores + logit_shift[0]) - diagonal)).astype(jnp.bfloat16)
        image_piece = jnp.dot(pair_coef, text_emb, preferred_element_type=jnp.float32)
        text_carry = text_carry + lax.dot_general(pair_coef, image_block, (((0,), (0,)), ((), ())), preferred_element_type=jnp.float32)
        return (text_carry, image_piece)
    text_unit_back, image_pieces = lax.scan(block_step, jnp.zeros((PAIRS, D), jnp.float32), jnp.arange(block_count, dtype=jnp.int32))
    image_unit_back = image_pieces.reshape(PAIRS, D)
    image_back = (image_unit_back - image_unit * lax.optimization_barrier(jnp.sum(image_unit * image_unit_back, axis=1, keepdims=True))) * image_invnorm
    hidden_back = lax.dot_general(image_back.astype(jnp.bfloat16), image_down, (((1,), (1,)), ((), ())), preferred_element_type=jnp.float32)
    pre_back = (hidden_back * hidden_slope).astype(jnp.bfloat16)
    ready_back = lax.dot_general(pre_back, image_up, (((1,), (1,)), ((), ())), preferred_element_type=jnp.float32)
    image_grad = image_back + norm_backward(ready_back, image_normed, image_inverse, image_norm_gain)
    text_back = (text_unit_back - text_unit * lax.optimization_barrier(jnp.sum(text_unit * text_unit_back, axis=1, keepdims=True))) * text_invnorm
    column_back = lax.dot_general(text_back.astype(jnp.bfloat16), text_head, (((1,), (1,)), ((), ())), preferred_element_type=jnp.float32)
    text_grad = norm_backward(column_back, text_normed, text_inverse, text_norm_gain)
    return (image_grad, text_grad)
```

```python
import jax
import jax.numpy as jnp
from jax import lax
from jax.sharding import Mesh, PartitionSpec as P

epsilon = 1e-06
tanh_coef = 0.7978845608028654
cubic_coef = 0.044715
low = jnp.bfloat16
DP = ("ylo", "x", "z", "core")
GROUP = ("ylo", "x", "core")


def gelu_parts(preact):
    inside = tanh_coef * (preact + cubic_coef * preact * preact * preact)
    tangent = jnp.tanh(inside)
    activated = 0.5 * preact * (1.0 + tangent)
    derivative = 0.5 * (1.0 + tangent) + 0.5 * preact * (1.0 - tangent * tangent) * tanh_coef * (
        1.0 + 3.0 * cubic_coef * preact * preact
    )
    return (activated, derivative)


def norm_stats(source):
    centre = source - jnp.mean(source, axis=1, keepdims=True)
    inverse = lax.rsqrt(jnp.mean(centre * centre, axis=1, keepdims=True) + epsilon)
    return (centre * inverse, inverse)


def norm_backward(upstream, normed, inverse, gain_vec):
    scaled = upstream * gain_vec
    return inverse * (
        scaled
        - jnp.mean(scaled, axis=1, keepdims=True)
        - normed * jnp.mean(scaled * normed, axis=1, keepdims=True)
    )


def unit_rows(total):
    inverse = lax.rsqrt(jnp.sum(total * total, axis=1, keepdims=True) + epsilon)
    return (total * inverse, inverse)


def unit_backward(upstream, unit, inverse):
    return (upstream - unit * jnp.sum(unit * upstream, axis=1, keepdims=True)) * inverse


def mm(a, b):
    return jnp.dot(a, b, preferred_element_type=jnp.float32)


def mm_nt(a, b):
    return lax.dot_general(a, b, (((1,), (1,)), ((), ())), preferred_element_type=jnp.float32)


def mm_tn(a, b):
    return lax.dot_general(a, b, (((0,), (0,)), ((), ())), preferred_element_type=jnp.float32)


def spread(block, axes):
    count = lax.axis_size(axes)
    slots = jnp.broadcast_to(block[None], (count,) + block.shape)
    return lax.all_to_all(slots, axes, 0, 0, tiled=True)


def sum_slots(partial, axes):
    count = lax.axis_size(axes)
    slots = partial.astype(low).reshape(count, partial.shape[0] // count, partial.shape[1])
    return jnp.sum(lax.all_to_all(slots, axes, 0, 0, tiled=True).astype(jnp.float32), axis=0)


def tensor_total(partial):
    count = lax.axis_size("tensor")
    sent = partial.astype(low)
    total = sent.astype(jnp.float32)
    for step in range(1, count):
        turn = [(i, (i + step) % count) for i in range(count)]
        total = total + lax.ppermute(sent, "tensor", turn).astype(jnp.float32)
    return total


def per_device(
    image_pooled,
    text_pooled,
    image_norm_gain,
    image_norm_bias,
    image_up,
    image_up_bias,
    image_down,
    image_down_bias,
    text_norm_gain,
    text_norm_bias,
    text_head,
    text_head_bias,
    log_scale,
    logit_shift,
    loss_scale,
):
    ylo_count, x_count, z_count, core_count = (lax.axis_size(a) for a in DP)
    tensor_count = lax.axis_size("tensor")
    group_count = lax.axis_size(GROUP)
    tensor_rank = lax.axis_index("tensor")
    z_rank = lax.axis_index("z")
    group_rank = lax.axis_index(GROUP)
    block_rows, width = image_pooled.shape
    own_rows = block_rows // tensor_count
    pairs_total = block_rows * lax.axis_size(DP)
    slab, hidden_local = image_up.shape
    chunk = -(-hidden_local // (group_count * 4)) * 4
    hidden_mine = chunk * tensor_count

    def turned(vec):
        return (
            vec.reshape(ylo_count, x_count, z_count, core_count * slab).transpose(0, 2, 1, 3).reshape(width)
        )

    source_of = turned(jnp.arange(width, dtype=jnp.int32))
    turn = (jnp.arange(width, dtype=jnp.int32)[:, None] == source_of[None, :]).astype(low)

    def cut(arr):
        padded = jnp.pad(arr, ((0, 0), (0, chunk * group_count - hidden_local)))
        return padded.reshape(arr.shape[0], group_count, chunk)

    bias_high = image_up_bias.astype(low)
    bias_low = (image_up_bias - bias_high.astype(jnp.float32)).astype(low)
    rows = jnp.concatenate([image_up, image_down.T, bias_high[None], bias_low[None]], axis=0)
    slots = cut(rows).transpose(1, 0, 2)
    slots = jnp.broadcast_to(slots[:, None], (group_count, tensor_count) + slots.shape[1:])
    slots = slots.reshape((group_count * tensor_count,) + slots.shape[2:])
    got = lax.all_to_all(slots, GROUP + ("tensor",), 0, 0, tiled=True)
    got = got.reshape(ylo_count, x_count * core_count, tensor_count, 2 * slab + 2, chunk)
    up_bias = (
        got[0, 0, :, 2 * slab].astype(jnp.float32) + got[0, 0, :, 2 * slab + 1].astype(jnp.float32)
    ).reshape(hidden_mine)
    both = got[:, :, :, : 2 * slab].reshape(ylo_count, x_count * core_count, tensor_count, 2, slab, chunk)
    both = both.transpose(0, 1, 4, 3, 2, 5).reshape(
        ylo_count, x_count * core_count * slab, 2 * hidden_mine
    )
    first = spread(both[0], "z").reshape(-1, 2 * hidden_mine)
    second = lax.all_gather(both[1], "z", axis=0, tiled=True)
    weights = jnp.concatenate([first, second], axis=0)
    up_mine = weights[:, :hidden_mine]
    down_mine = weights[:, hidden_mine:]

    gain_turned = turned(image_norm_gain)
    image_own = lax.dynamic_slice_in_dim(image_pooled, tensor_rank * own_rows, own_rows, 0)
    image_own = mm(image_own, turn)
    image_normed, image_inverse = norm_stats(image_own)
    ready = (image_normed * gain_turned + turned(image_norm_bias)).astype(low)
    ready_all = lax.all_gather(ready, GROUP, axis=0, tiled=True)

    text_normed, text_inverse = norm_stats(text_pooled.astype(jnp.float32))
    text_ready = (text_normed * text_norm_gain + text_norm_bias).astype(low)
    head_rows = text_head.shape[0]
    text_columns = lax.dynamic_slice_in_dim(text_ready, tensor_rank * head_rows, head_rows, 1)
    head_turned = mm(text_head, turn).astype(low)
    text_sum = tensor_total(mm(text_columns, head_turned)) + turned(text_head_bias)
    text_unit, text_invnorm = unit_rows(text_sum)
    text_all = lax.all_gather(text_unit.astype(low), "z", axis=0, tiled=True)

    hidden_pre = mm(ready_all, up_mine) + up_bias
    hidden_act, hidden_slope = gelu_parts(hidden_pre)
    image_sum = sum_slots(mm_nt(hidden_act.astype(low), down_mine), GROUP)
    image_sum = image_sum + image_own + turned(image_down_bias)
    image_unit, image_invnorm = unit_rows(image_sum)
    image_all = spread(image_unit.astype(low), GROUP).reshape(-1, width)

    scale_value = jnp.exp(log_scale[0])
    factor = loss_scale[0] * scale_value / pairs_total
    scores = mm_nt(image_all, text_all)
    image_at = lax.broadcasted_iota(jnp.int32, scores.shape, 0) - group_rank * own_rows
    text_at = lax.broadcasted_iota(jnp.int32, scores.shape, 1) - (
        z_rank * block_rows + tensor_rank * own_rows
    )
    same = (image_at == text_at) & (image_at >= 0) & (image_at < own_rows)
    pair_coef = (
        factor * (jax.nn.sigmoid(scale_value * scores + logit_shift[0]) - same.astype(jnp.float32))
    ).astype(low)
    image_unit_back = sum_slots(mm(pair_coef, text_all), GROUP)
    text_part = mm_tn(pair_coef, image_all).astype(low)
    text_unit_back = tensor_total(lax.psum_scatter(text_part, "z", scatter_dimension=0, tiled=True))

    image_back = unit_backward(image_unit_back, image_unit, image_invnorm)
    back_all = spread(image_back.astype(low), GROUP).reshape(-1, width)
    pre_back = (mm(back_all, down_mine) * hidden_slope).astype(low)
    ready_back = sum_slots(mm_nt(pre_back, up_mine), GROUP)
    image_grad = image_back + norm_backward(ready_back, image_normed, image_inverse, gain_turned)
    image_grad = mm_nt(image_grad.astype(low), turn).astype(low)
    image_grad = spread(image_grad, "tensor").reshape(block_rows, width).astype(jnp.float32)

    text_back = unit_backward(text_unit_back, text_unit, text_invnorm)
    column_part = mm_nt(text_back.astype(low), head_turned).astype(low)
    column_back = spread(column_part, "tensor").transpose(1, 0, 2).reshape(block_rows, width)
    text_grad = norm_backward(column_back.astype(jnp.float32), text_normed, text_inverse, text_norm_gain)
    return (image_grad, text_grad)


def solution(mesh):
    grid = Mesh(mesh.devices.reshape(2, 4, 8, 2, 4), DP + ("tensor",))
    return jax.shard_map(
        per_device,
        mesh=grid,
        in_specs=(
            P(DP, None),
            P(DP, None),
            P(),
            P(),
            P(DP, "tensor"),
            P("tensor"),
            P("tensor", DP),
            P(),
            P(),
            P(),
            P("tensor", None),
            P(),
            P(),
            P(),
            P(),
        ),
        out_specs=(P(DP, None), P(DP, None)),
        check_vma=False,
    )
```

```python
import jax
import jax.numpy as jnp
from jax import lax
from jax.sharding import Mesh, PartitionSpec as P

epsilon = 1e-06
tanh_coef = 0.7978845608028654
cubic_coef = 0.044715
low = jnp.bfloat16
DP = ("ylo", "x", "z", "core")
GROUP = ("x", "ylo", "core")
IMAGES = ("z", "ylo")


def gelu_parts(preact):
    inside = tanh_coef * (preact + cubic_coef * preact * preact * preact)
    tangent = jnp.tanh(inside)
    activated = 0.5 * preact * (1.0 + tangent)
    derivative = 0.5 * (1.0 + tangent) + 0.5 * preact * (1.0 - tangent * tangent) * tanh_coef * (
        1.0 + 3.0 * cubic_coef * preact * preact
    )
    return (activated, derivative)


def norm_stats(source):
    centre = source - jnp.mean(source, axis=1, keepdims=True)
    inverse = lax.rsqrt(jnp.mean(centre * centre, axis=1, keepdims=True) + epsilon)
    return (centre * inverse, inverse)


def norm_backward(upstream, normed, inverse, gain_vec):
    scaled = upstream * gain_vec
    return inverse * (
        scaled
        - jnp.mean(scaled, axis=1, keepdims=True)
        - normed * jnp.mean(scaled * normed, axis=1, keepdims=True)
    )


def unit_rows(total):
    inverse = lax.rsqrt(jnp.sum(total * total, axis=1, keepdims=True) + epsilon)
    return (total * inverse, inverse)


def unit_backward(upstream, unit, inverse):
    return (upstream - unit * jnp.sum(unit * upstream, axis=1, keepdims=True)) * inverse


def mm(a, b):
    return jnp.dot(a, b, preferred_element_type=jnp.float32)


def mm_nt(a, b):
    return lax.dot_general(a, b, (((1,), (1,)), ((), ())), preferred_element_type=jnp.float32)


def mm_tn(a, b):
    return lax.dot_general(a, b, (((0,), (0,)), ((), ())), preferred_element_type=jnp.float32)


def spread(block, axes):
    count = lax.axis_size(axes)
    slots = jnp.broadcast_to(block[None], (count,) + block.shape)
    return lax.all_to_all(slots, axes, 0, 0, tiled=True)


def sum_slots(partial, axes):
    count = lax.axis_size(axes)
    slots = partial.astype(low).reshape(count, partial.shape[0] // count, partial.shape[1])
    return jnp.sum(lax.all_to_all(slots, axes, 0, 0, tiled=True).astype(jnp.float32), axis=0)


def passed(block, axis, step):
    count = lax.axis_size(axis)
    return lax.ppermute(block, axis, [(i, (i + step) % count) for i in range(count)])


def together(*values):
    return lax.optimization_barrier(values)


def tensor_total(sent, earlier):
    got = [passed(sent, "tensor", step) for step in range(1, lax.axis_size("tensor"))]
    got, earlier = lax.optimization_barrier((got, earlier))
    total = sent.astype(jnp.float32)
    for part in got:
        total = total + part.astype(jnp.float32)
    return (total, earlier)


def per_device(
    image_pooled,
    text_pooled,
    image_norm_gain,
    image_norm_bias,
    image_up,
    image_up_bias,
    image_down,
    image_down_bias,
    text_norm_gain,
    text_norm_bias,
    text_head,
    text_head_bias,
    log_scale,
    logit_shift,
    loss_scale,
):
    ylo_count, x_count, z_count, core_count = (lax.axis_size(a) for a in DP)
    tensor_count = lax.axis_size("tensor")
    group_count = lax.axis_size(GROUP)
    tensor_rank = lax.axis_index("tensor")
    block_rows, width = image_pooled.shape
    own_rows = block_rows // tensor_count
    pairs_total = block_rows * lax.axis_size(DP)
    slab, hidden_local = image_up.shape
    chunk = -(-hidden_local // (group_count * 4)) * 4
    hidden_mine = chunk * tensor_count

    def turned(vec):
        return (
            vec.reshape(ylo_count, x_count, z_count, core_count * slab).transpose(2, 1, 0, 3).reshape(width)
        )

    source_of = turned(jnp.arange(width, dtype=jnp.int32))
    turn = (jnp.arange(width, dtype=jnp.int32)[:, None] == source_of[None, :]).astype(low)

    def cut(arr):
        padded = jnp.pad(arr, ((0, 0), (0, chunk * group_count - hidden_local)))
        return padded.reshape(arr.shape[0], group_count, chunk)

    bias_high = image_up_bias.astype(low)
    bias_low = (image_up_bias - bias_high.astype(jnp.float32)).astype(low)
    rows = jnp.concatenate([image_up, image_down.T, bias_high[None], bias_low[None]], axis=0)
    slots = cut(rows).transpose(1, 0, 2)
    slots = jnp.broadcast_to(slots[:, None], (group_count, tensor_count) + slots.shape[1:])
    slots = slots.reshape((group_count * tensor_count,) + slots.shape[2:])
    got = lax.all_to_all(slots, GROUP + ("tensor",), 0, 0, tiled=True)
    gain_turned = turned(image_norm_gain)
    image_own = lax.dynamic_slice_in_dim(image_pooled, tensor_rank * own_rows, own_rows, 0)
    image_own = mm(image_own, turn)
    image_normed, image_inverse = norm_stats(image_own)
    ready = (image_normed * gain_turned + turned(image_norm_bias)).astype(low)
    ready_all = lax.all_gather(ready, ("ylo", "core"), axis=0, tiled=True)
    ready_all, got = lax.optimization_barrier((ready_all, got))
    ready_all = lax.all_gather(ready_all, "x", axis=0, tiled=True)

    text_float, got = lax.optimization_barrier((text_pooled, got))
    got = got.reshape(group_count, tensor_count, 2 * slab + 2, chunk)
    up_bias = (
        got[0, :, 2 * slab].astype(jnp.float32) + got[0, :, 2 * slab + 1].astype(jnp.float32)
    ).reshape(hidden_mine)
    both = got[:, :, : 2 * slab].reshape(group_count, tensor_count, 2, slab, chunk)
    both = both.transpose(0, 3, 2, 1, 4).reshape(group_count * slab, 2 * hidden_mine)
    weights = spread(both, "z").reshape(width, 2 * hidden_mine)

    text_normed, text_inverse = norm_stats(text_float.astype(jnp.float32))
    text_ready = (text_normed * text_norm_gain + text_norm_bias).astype(low)
    head_rows = text_head.shape[0]
    text_columns = lax.dynamic_slice_in_dim(text_ready, tensor_rank * head_rows, head_rows, 1)
    head_turned = mm(text_head, turn).astype(low)
    text_sent = mm(text_columns, head_turned).astype(low)
    text_total, ready_all = tensor_total(text_sent, ready_all)
    text_unit, text_invnorm = unit_rows(text_total + turned(text_head_bias))
    text_emb = text_unit.astype(low)
    ready_all, text_emb = together(ready_all, text_emb)
    up_mine = weights[:, :hidden_mine]
    down_mine = weights[:, hidden_mine:]

    hidden_pre = mm(ready_all, up_mine) + up_bias
    hidden_act, hidden_slope = gelu_parts(hidden_pre)
    image_part = mm_nt(hidden_act.astype(low), down_mine).astype(low)
    image_part, text_emb = together(image_part, text_emb)
    x_steps = range(1, lax.axis_size("x"))
    image_sum, text_near = together(
        sum_slots(image_part, GROUP),
        [text_emb] + [passed(text_emb, "x", step) for step in x_steps],
    )
    text_near = jnp.concatenate(text_near, axis=0)
    image_sum = image_sum + image_own + turned(image_down_bias)
    image_unit, image_invnorm = unit_rows(image_sum)
    image_all, text_far = together(
        spread(image_unit.astype(low), IMAGES).reshape(-1, width), passed(text_near, "core", 1)
    )
    text_all = jnp.concatenate([text_near, text_far], axis=0)

    scale_value = jnp.exp(log_scale[0])
    factor = loss_scale[0] * scale_value / pairs_total
    scores = mm_nt(image_all, text_all)
    image_at = lax.broadcasted_iota(jnp.int32, scores.shape, 0) - lax.axis_index(IMAGES) * own_rows
    text_at = lax.broadcasted_iota(jnp.int32, scores.shape, 1) - tensor_rank * own_rows
    same = (image_at == text_at) & (image_at >= 0) & (image_at < own_rows)
    pair_coef = (
        factor * (jax.nn.sigmoid(scale_value * scores + logit_shift[0]) - same.astype(jnp.float32))
    ).astype(low)
    text_part = mm_tn(pair_coef, image_all).astype(low)
    pair_coef, text_part = together(pair_coef, text_part)
    near_rows = text_near.shape[0]
    text_part = text_part[:near_rows].astype(jnp.float32) + passed(
        text_part[near_rows:], "core", 1
    ).astype(jnp.float32)
    text_part = text_part.astype(low).reshape(-1, block_rows, width)
    image_unit_back, text_got = together(
        sum_slots(mm(pair_coef, text_all), IMAGES),
        [text_part[0]] + [passed(text_part[step], "x", -step) for step in x_steps],
    )
    text_unit_back = sum(part.astype(jnp.float32) for part in text_got).astype(low)

    image_back = unit_backward(image_unit_back, image_unit, image_invnorm)
    back_all = spread(image_back.astype(low), GROUP).reshape(-1, width)
    pre_back = (mm(back_all, down_mine) * hidden_slope).astype(low)
    ready_sent = mm_nt(pre_back, up_mine).astype(low)
    text_unit_back, ready_sent = tensor_total(text_unit_back, ready_sent)
    ready_back = sum_slots(ready_sent, GROUP)
    image_grad = image_back + norm_backward(ready_back, image_normed, image_inverse, gain_turned)
    image_low = mm_nt(image_grad.astype(low), turn).astype(low)

    text_back = unit_backward(text_unit_back, text_unit, text_invnorm)
    lanes = 128
    head_tiles = -(-head_rows // lanes)
    head_padded = jnp.pad(head_turned, ((0, head_tiles * lanes - head_rows), (0, 0)))
    column_part = mm_nt(text_back.astype(low), head_padded).astype(low)

    tiles = width // lanes
    last = jnp.concatenate(
        [
            image_low.reshape(own_rows, tiles, lanes).transpose(1, 0, 2).reshape(-1, lanes),
            column_part.reshape(block_rows, head_tiles, lanes).transpose(1, 0, 2).reshape(-1, lanes),
        ],
        axis=0,
    )
    last = spread(last, "tensor")
    image_grad = last[:, : tiles * own_rows].reshape(tensor_count, tiles, own_rows, lanes)
    image_grad = image_grad.transpose(0, 2, 1, 3).reshape(block_rows, width).astype(jnp.float32)
    column_back = last[:, tiles * own_rows :].reshape(tensor_count, head_tiles, block_rows, lanes)
    column_back = column_back.transpose(2, 0, 1, 3).reshape(block_rows, tensor_count, head_tiles * lanes)
    column_back = column_back[:, :, :head_rows].reshape(block_rows, width)
    text_grad = norm_backward(column_back.astype(jnp.float32), text_normed, text_inverse, text_norm_gain)
    return (image_grad, text_grad)


def solution(mesh):
    grid = Mesh(mesh.devices.reshape(2, 4, 8, 2, 4), DP + ("tensor",))
    return jax.shard_map(
        per_device,
        mesh=grid,
        in_specs=(
            P(DP, None),
            P(DP, None),
            P(),
            P(),
            P(DP, "tensor"),
            P("tensor"),
            P("tensor", DP),
            P(),
            P(),
            P(),
            P("tensor", None),
            P(),
            P(),
            P(),
            P(),
        ),
        out_specs=(P(DP, None), P(DP, None)),
        check_vma=False,
    )
```

```python
import jax
import jax.numpy as jnp
from jax import lax
from jax.experimental import pallas as pl
from jax.experimental.pallas import tpu as pltpu
from jax.sharding import Mesh, PartitionSpec as P

epsilon = 1e-06
tanh_coef = 0.7978845608028654
cubic_coef = 0.044715
low = jnp.bfloat16
DP = ("ylo", "x", "z", "core")
GROUP = ("x", "ylo", "core")
IMAGES = ("z", "ylo")


def gelu_parts(preact):
    inside = tanh_coef * (preact + cubic_coef * preact * preact * preact)
    tangent = jnp.tanh(inside)
    activated = 0.5 * preact * (1.0 + tangent)
    derivative = 0.5 * (1.0 + tangent) + 0.5 * preact * (1.0 - tangent * tangent) * tanh_coef * (
        1.0 + 3.0 * cubic_coef * preact * preact
    )
    return (activated, derivative)


def norm_stats(source):
    centre = source - jnp.mean(source, axis=1, keepdims=True)
    inverse = lax.rsqrt(jnp.mean(centre * centre, axis=1, keepdims=True) + epsilon)
    return (centre * inverse, inverse)


def norm_backward(upstream, normed, inverse, gain_vec):
    scaled = upstream * gain_vec
    return inverse * (
        scaled
        - jnp.mean(scaled, axis=1, keepdims=True)
        - normed * jnp.mean(scaled * normed, axis=1, keepdims=True)
    )


def unit_rows(total):
    inverse = lax.rsqrt(jnp.sum(total * total, axis=1, keepdims=True) + epsilon)
    return (total * inverse, inverse)


def unit_backward(upstream, unit, inverse):
    return (upstream - unit * jnp.sum(unit * upstream, axis=1, keepdims=True)) * inverse


def mm(a, b):
    return jnp.dot(a, b, preferred_element_type=jnp.float32)


def mm_nt(a, b):
    return lax.dot_general(a, b, (((1,), (1,)), ((), ())), preferred_element_type=jnp.float32)


def mm_tn(a, b):
    return lax.dot_general(a, b, (((0,), (0,)), ((), ())), preferred_element_type=jnp.float32)


def spread(block, axes):
    count = lax.axis_size(axes)
    slots = jnp.broadcast_to(block[None], (count,) + block.shape)
    return lax.all_to_all(slots, axes, 0, 0, tiled=True)


def swap_slots(partial, axes):
    count = lax.axis_size(axes)
    slots = partial.astype(low).reshape(count, partial.shape[0] // count, partial.shape[1])
    return lax.all_to_all(slots, axes, 0, 0, tiled=True)


def sum_slots(partial, axes):
    return jnp.sum(swap_slots(partial, axes).astype(jnp.float32), axis=0)


def passed(block, axis, step):
    count = lax.axis_size(axis)
    return lax.ppermute(block, axis, [(i, (i + step) % count) for i in range(count)])


def together(*values):
    return lax.optimization_barrier(values)


def tensor_total(sent, earlier):
    got = [passed(sent, "tensor", step) for step in range(1, lax.axis_size("tensor"))]
    got, earlier = lax.optimization_barrier((got, earlier))
    total = sent.astype(jnp.float32)
    for part in got:
        total = total + part.astype(jnp.float32)
    return (total, earlier)


def pair_kernel(number_ref, place_ref, image_ref, near_ref, far_ref, near_coef_ref, far_coef_ref, part_ref):
    scale_value, shift, factor = (number_ref[i] for i in range(3))
    image = image_ref[...]
    near = near_ref[...]
    far = far_ref[...]
    chance = jax.nn.sigmoid(scale_value * mm_nt(image, near) + shift)
    image_at = lax.broadcasted_iota(jnp.int32, chance.shape, 0) - place_ref[0]
    text_at = lax.broadcasted_iota(jnp.int32, chance.shape, 1) - place_ref[1]
    same = (image_at == text_at) & (image_at >= 0) & (image_at < place_ref[2])
    near_coef = (factor * (chance - same.astype(jnp.float32))).astype(low)
    far_coef = (factor * jax.nn.sigmoid(scale_value * mm_nt(image, far) + shift)).astype(low)
    near_coef_ref[...] = near_coef
    far_coef_ref[...] = far_coef
    part_ref[...] = (mm(near_coef, near) + mm(far_coef, far)).astype(low)


def back_kernel(got_ref, unit_ref, inverse_ref, back_ref, slots_ref):
    upstream = jnp.sum(got_ref[...].astype(jnp.float32), axis=0)
    back = unit_backward(upstream, unit_ref[...], inverse_ref[...])
    back_ref[...] = back
    sent = back.astype(low)
    for slot in range(slots_ref.shape[0]):
        slots_ref[slot] = sent


def back_slots(got, unit, inverse, count):
    vmem = pl.BlockSpec(memory_space=pltpu.VMEM)
    return pl.pallas_call(
        back_kernel,
        out_shape=(
            jax.ShapeDtypeStruct(unit.shape, jnp.float32),
            jax.ShapeDtypeStruct((count,) + unit.shape, low),
        ),
        in_specs=[vmem, vmem, vmem],
        out_specs=(vmem, vmem),
        compiler_params=pltpu.CompilerParams(vmem_limit_bytes=10 * 1024 * 1024),
    )(got, unit, inverse)


def pairs(numbers, places, image, near, far):
    rows, width = image.shape
    vmem, smem = pl.BlockSpec(memory_space=pltpu.VMEM), pl.BlockSpec(memory_space=pltpu.SMEM)
    return pl.pallas_call(
        pair_kernel,
        out_shape=(
            jax.ShapeDtypeStruct((rows, near.shape[0]), low),
            jax.ShapeDtypeStruct((rows, far.shape[0]), low),
            jax.ShapeDtypeStruct((rows, width), low),
        ),
        in_specs=[smem, smem, vmem, vmem, vmem],
        out_specs=(vmem, vmem, vmem),
        compiler_params=pltpu.CompilerParams(vmem_limit_bytes=10 * 1024 * 1024),
    )(numbers, places, image, near, far)


def per_device(
    image_pooled,
    text_pooled,
    image_norm_gain,
    image_norm_bias,
    image_up,
    image_up_bias,
    image_down,
    image_down_bias,
    text_norm_gain,
    text_norm_bias,
    text_head,
    text_head_bias,
    log_scale,
    logit_shift,
    loss_scale,
):
    ylo_count, x_count, z_count, core_count = (lax.axis_size(a) for a in DP)
    tensor_count = lax.axis_size("tensor")
    group_count = lax.axis_size(GROUP)
    tensor_rank = lax.axis_index("tensor")
    block_rows, width = image_pooled.shape
    own_rows = block_rows // tensor_count
    pairs_total = block_rows * lax.axis_size(DP)
    slab, hidden_local = image_up.shape
    chunk = -(-hidden_local // (group_count * 4)) * 4
    hidden_mine = chunk * tensor_count

    def turned(vec):
        return (
            vec.reshape(ylo_count, x_count, z_count, core_count * slab).transpose(2, 1, 0, 3).reshape(width)
        )

    source_of = turned(jnp.arange(width, dtype=jnp.int32))
    turn = (jnp.arange(width, dtype=jnp.int32)[:, None] == source_of[None, :]).astype(low)

    def cut(arr):
        padded = jnp.pad(arr, ((0, 0), (0, chunk * group_count - hidden_local)))
        return padded.reshape(arr.shape[0], group_count, chunk)

    bias_high = image_up_bias.astype(low)
    bias_low = (image_up_bias - bias_high.astype(jnp.float32)).astype(low)
    rows = jnp.concatenate([image_up, image_down.T, bias_high[None], bias_low[None]], axis=0)
    slots = cut(rows).transpose(1, 0, 2)
    slots = jnp.broadcast_to(slots[:, None], (group_count, tensor_count) + slots.shape[1:])
    slots = slots.reshape((group_count * tensor_count,) + slots.shape[2:])
    got = lax.all_to_all(slots, GROUP + ("tensor",), 0, 0, tiled=True)
    gain_turned = turned(image_norm_gain)
    image_own = lax.dynamic_slice_in_dim(image_pooled, tensor_rank * own_rows, own_rows, 0)
    image_own = mm(image_own, turn)
    image_normed, image_inverse = norm_stats(image_own)
    ready = (image_normed * gain_turned + turned(image_norm_bias)).astype(low)
    ready_all = lax.all_gather(ready, ("ylo", "core"), axis=0, tiled=True)
    ready_all, got = lax.optimization_barrier((ready_all, got))
    ready_all = lax.all_gather(ready_all, "x", axis=0, tiled=True)

    text_float, got = lax.optimization_barrier((text_pooled, got))
    got = got.reshape(group_count, tensor_count, 2 * slab + 2, chunk)
    up_bias = (
        got[0, :, 2 * slab].astype(jnp.float32) + got[0, :, 2 * slab + 1].astype(jnp.float32)
    ).reshape(hidden_mine)
    both = got[:, :, : 2 * slab].reshape(group_count, tensor_count, 2, slab, chunk)
    both = both.transpose(0, 3, 2, 1, 4).reshape(group_count * slab, 2 * hidden_mine)
    weights = spread(both, "z").reshape(width, 2 * hidden_mine)

    text_normed, text_inverse = norm_stats(text_float.astype(jnp.float32))
    text_ready = (text_normed * text_norm_gain + text_norm_bias).astype(low)
    head_rows = text_head.shape[0]
    text_columns = lax.dynamic_slice_in_dim(text_ready, tensor_rank * head_rows, head_rows, 1)
    head_turned = mm(text_head, turn).astype(low)
    text_sent = mm(text_columns, head_turned).astype(low)
    text_total, ready_all = tensor_total(text_sent, ready_all)
    text_unit, text_invnorm = unit_rows(text_total + turned(text_head_bias))
    text_emb = text_unit.astype(low)
    ready_all, text_emb = together(ready_all, text_emb)
    up_mine = weights[:, :hidden_mine]
    down_mine = weights[:, hidden_mine:]

    hidden_pre = mm(ready_all, up_mine) + up_bias
    hidden_act, hidden_slope = gelu_parts(hidden_pre)
    image_part = mm_nt(hidden_act.astype(low), down_mine).astype(low)
    x_steps = range(1, lax.axis_size("x"))
    image_part, text_emb, text_got = together(image_part, text_emb, passed(text_emb, "x", 2))
    image_sum, text_near = together(
        sum_slots(image_part, GROUP),
        [text_emb, passed(text_emb, "x", 1), text_got, passed(text_emb, "x", 3)],
    )
    text_near = jnp.concatenate(text_near, axis=0)
    image_sum = image_sum + image_own + turned(image_down_bias)
    image_unit, image_invnorm = unit_rows(image_sum)
    image_all, text_far = together(
        spread(image_unit.astype(low), IMAGES).reshape(-1, width), passed(text_near, "core", 1)
    )

    scale_value = jnp.exp(log_scale[0])
    numbers = jnp.stack([scale_value, logit_shift[0], loss_scale[0] * scale_value / pairs_total])
    places = jnp.stack(
        [lax.axis_index(IMAGES) * own_rows, tensor_rank * own_rows, jnp.int32(own_rows)]
    ).astype(jnp.int32)
    near_coef, far_coef, image_part = pairs(numbers, places, image_all, text_near, text_far)
    far_part = mm_tn(far_coef, image_all).astype(low)
    text_part = mm_tn(near_coef, image_all) + passed(far_part, "core", 1).astype(jnp.float32)
    text_part = text_part.astype(low).reshape(-1, block_rows, width)
    image_got, text_got = together(
        swap_slots(image_part, IMAGES),
        [text_part[0]] + [passed(text_part[step], "x", -step) for step in x_steps],
    )
    text_unit_back = sum(part.astype(jnp.float32) for part in text_got).astype(low)

    image_back, slots = back_slots(image_got, image_unit, image_invnorm, group_count)
    back_all = lax.all_to_all(slots, GROUP, 0, 0, tiled=True).reshape(-1, width)
    pre_back = (mm(back_all, down_mine) * hidden_slope).astype(low)
    ready_sent = mm_nt(pre_back, up_mine).astype(low)
    text_got = [text_unit_back] + [passed(text_unit_back, "tensor", step) for step in (1, 2, 3)]
    ready_sent, text_got[1], text_got[3] = together(ready_sent, text_got[1], text_got[3])
    ready_back, text_got[2] = together(sum_slots(ready_sent, GROUP), text_got[2])
    text_unit_back = sum(part.astype(jnp.float32) for part in text_got)
    image_grad = image_back + norm_backward(ready_back, image_normed, image_inverse, gain_turned)
    image_low = mm_nt(image_grad.astype(low), turn).astype(low)

    text_back = unit_backward(text_unit_back, text_unit, text_invnorm)
    lanes = 128
    head_tiles = -(-head_rows // lanes)
    head_padded = jnp.pad(head_turned, ((0, head_tiles * lanes - head_rows), (0, 0)))
    column_part = mm_nt(text_back.astype(low), head_padded).astype(low)

    tiles = width // lanes
    last = jnp.concatenate(
        [
            image_low.reshape(own_rows, tiles, lanes).transpose(1, 0, 2).reshape(-1, lanes),
            column_part.reshape(block_rows, head_tiles, lanes).transpose(1, 0, 2).reshape(-1, lanes),
        ],
        axis=0,
    )
    last = spread(last, "tensor")
    image_grad = last[:, : tiles * own_rows].reshape(tensor_count, tiles, own_rows, lanes)
    image_grad = image_grad.transpose(0, 2, 1, 3).reshape(block_rows, width).astype(jnp.float32)
    column_back = last[:, tiles * own_rows :].reshape(tensor_count, head_tiles, block_rows, lanes)
    column_back = column_back.transpose(2, 0, 1, 3).reshape(block_rows, tensor_count, head_tiles * lanes)
    column_back = column_back[:, :, :head_rows].reshape(block_rows, width)
    text_grad = norm_backward(column_back.astype(jnp.float32), text_normed, text_inverse, text_norm_gain)
    return (image_grad, text_grad)


def solution(mesh):
    grid = Mesh(mesh.devices.reshape(2, 4, 8, 2, 4), DP + ("tensor",))
    return jax.shard_map(
        per_device,
        mesh=grid,
        in_specs=(
            P(DP, None),
            P(DP, None),
            P(),
            P(),
            P(DP, "tensor"),
            P("tensor"),
            P("tensor", DP),
            P(),
            P(),
            P(),
            P("tensor", None),
            P(),
            P(),
            P(),
            P(),
        ),
        out_specs=(P(DP, None), P(DP, None)),
        check_vma=False,
    )
```

```python
import jax
import jax.numpy as jnp
from jax import lax
from jax.experimental import pallas as pl
from jax.experimental.pallas import tpu as pltpu
from jax.sharding import Mesh, PartitionSpec as P

epsilon = 1e-06
tanh_coef = 0.7978845608028654
cubic_coef = 0.044715
low = jnp.bfloat16
lanes = 128
DP = ("ylo", "x", "z", "core")
GROUP = ("x", "ylo", "core")
IMAGES = ("z", "ylo")


def gelu_parts(preact):
    inside = tanh_coef * (preact + cubic_coef * preact * preact * preact)
    tangent = jnp.tanh(inside)
    activated = 0.5 * preact * (1.0 + tangent)
    derivative = 0.5 * (1.0 + tangent) + 0.5 * preact * (1.0 - tangent * tangent) * tanh_coef * (
        1.0 + 3.0 * cubic_coef * preact * preact
    )
    return (activated, derivative)


def norm_stats(source):
    centre = source - jnp.mean(source, axis=1, keepdims=True)
    inverse = lax.rsqrt(jnp.mean(centre * centre, axis=1, keepdims=True) + epsilon)
    return (centre * inverse, inverse)


def norm_backward(upstream, normed, inverse, gain_vec):
    scaled = upstream * gain_vec
    return inverse * (
        scaled
        - jnp.mean(scaled, axis=1, keepdims=True)
        - normed * jnp.mean(scaled * normed, axis=1, keepdims=True)
    )


def unit_rows(total):
    inverse = lax.rsqrt(jnp.sum(total * total, axis=1, keepdims=True) + epsilon)
    return (total * inverse, inverse)


def unit_backward(upstream, unit, inverse):
    return (upstream - unit * jnp.sum(unit * upstream, axis=1, keepdims=True)) * inverse


def mm(a, b):
    return jnp.dot(a, b, preferred_element_type=jnp.float32)


def mm_nt(a, b):
    return lax.dot_general(a, b, (((1,), (1,)), ((), ())), preferred_element_type=jnp.float32)


def mm_tn(a, b):
    return lax.dot_general(a, b, (((0,), (0,)), ((), ())), preferred_element_type=jnp.float32)


def spread(block, axes):
    count = lax.axis_size(axes)
    slots = jnp.broadcast_to(block[None], (count,) + block.shape)
    return lax.all_to_all(slots, axes, 0, 0, tiled=True)


def swap_slots(partial, axes):
    count = lax.axis_size(axes)
    slots = partial.astype(low).reshape(count, partial.shape[0] // count, partial.shape[1])
    return lax.all_to_all(slots, axes, 0, 0, tiled=True)


def sum_slots(partial, axes):
    return jnp.sum(swap_slots(partial, axes).astype(jnp.float32), axis=0)


def passed(block, axis, step):
    count = lax.axis_size(axis)
    return lax.ppermute(block, axis, [(i, (i + step) % count) for i in range(count)])


def crossed(block, axis, bits):
    return lax.ppermute(block, axis, [(i, i ^ bits) for i in range(lax.axis_size(axis))])


def add(one, other):
    return (one.astype(jnp.float32) + other.astype(jnp.float32)).astype(low)


def together(*values):
    return lax.optimization_barrier(values)


def tensor_total(sent, earlier):
    got = [passed(sent, "tensor", step) for step in range(1, lax.axis_size("tensor"))]
    got, earlier = lax.optimization_barrier((got, earlier))
    total = sent.astype(jnp.float32)
    for part in got:
        total = total + part.astype(jnp.float32)
    return (total, earlier)


def pair_kernel(number_ref, place_ref, image_ref, near_ref, far_ref, near_coef_ref, far_coef_ref, part_ref):
    scale_value, shift, factor = (number_ref[i] for i in range(3))
    image = image_ref[...]
    near = near_ref[...]
    far = far_ref[...]
    chance = jax.nn.sigmoid(scale_value * mm_nt(image, near) + shift)
    image_at = lax.broadcasted_iota(jnp.int32, chance.shape, 0) - place_ref[0]
    text_at = lax.broadcasted_iota(jnp.int32, chance.shape, 1) - place_ref[1]
    same = (image_at == text_at) & (image_at >= 0) & (image_at < place_ref[2])
    near_coef = (factor * (chance - same.astype(jnp.float32))).astype(low)
    far_coef = (factor * jax.nn.sigmoid(scale_value * mm_nt(image, far) + shift)).astype(low)
    near_coef_ref[...] = near_coef
    far_coef_ref[...] = far_coef
    part_ref[...] = (mm(near_coef, near) + mm(far_coef, far)).astype(low)


def back_kernel(got_ref, unit_ref, inverse_ref, back_ref, slots_ref):
    upstream = jnp.sum(got_ref[...].astype(jnp.float32), axis=0)
    back = unit_backward(upstream, unit_ref[...], inverse_ref[...])
    back_ref[...] = back
    sent = back.astype(low)
    for slot in range(slots_ref.shape[0]):
        slots_ref[slot] = sent


def back_slots(got, unit, inverse, count):
    vmem = pl.BlockSpec(memory_space=pltpu.VMEM)
    return pl.pallas_call(
        back_kernel,
        out_shape=(
            jax.ShapeDtypeStruct(unit.shape, jnp.float32),
            jax.ShapeDtypeStruct((count,) + unit.shape, low),
        ),
        in_specs=[vmem, vmem, vmem],
        out_specs=(vmem, vmem),
        compiler_params=pltpu.CompilerParams(vmem_limit_bytes=10 * 1024 * 1024),
    )(got, unit, inverse)


def output_kernel(last_ref, normed_ref, inverse_ref, gain_ref, image_ref, text_ref):
    count = last_ref.shape[0]
    rows, width = image_ref.shape
    own, tiles = rows // count, width // lanes
    for slot in range(count):
        for tile in range(tiles):
            image_ref[slot * own : (slot + 1) * own, tile * lanes : (tile + 1) * lanes] = last_ref[
                slot, tile * own : (tile + 1) * own
            ].astype(jnp.float32)
    pieces = []
    for slot in range(count):
        left = width // count
        for at in range(tiles * own, last_ref.shape[1], rows):
            piece = last_ref[slot, at : at + rows].astype(jnp.float32)
            pieces.append(piece[:, : min(left, lanes)])
            left -= lanes
    column_back = jnp.concatenate(pieces, axis=1)
    text_ref[...] = norm_backward(column_back, normed_ref[...], inverse_ref[...], gain_ref[...])


def outputs(last, normed, inverse, gain):
    vmem = pl.BlockSpec(memory_space=pltpu.VMEM)
    return pl.pallas_call(
        output_kernel,
        out_shape=(jax.ShapeDtypeStruct(normed.shape, jnp.float32),) * 2,
        in_specs=[vmem] * 4,
        out_specs=(vmem, vmem),
        compiler_params=pltpu.CompilerParams(vmem_limit_bytes=10 * 1024 * 1024),
    )(last, normed, inverse, gain)


def pairs(numbers, places, image, near, far):
    rows, width = image.shape
    vmem, smem = pl.BlockSpec(memory_space=pltpu.VMEM), pl.BlockSpec(memory_space=pltpu.SMEM)
    return pl.pallas_call(
        pair_kernel,
        out_shape=(
            jax.ShapeDtypeStruct((rows, near.shape[0]), low),
            jax.ShapeDtypeStruct((rows, far.shape[0]), low),
            jax.ShapeDtypeStruct((rows, width), low),
        ),
        in_specs=[smem, smem, vmem, vmem, vmem],
        out_specs=(vmem, vmem, vmem),
        compiler_params=pltpu.CompilerParams(vmem_limit_bytes=10 * 1024 * 1024),
    )(numbers, places, image, near, far)


def per_device(
    image_pooled,
    text_pooled,
    image_norm_gain,
    image_norm_bias,
    image_up,
    image_up_bias,
    image_down,
    image_down_bias,
    text_norm_gain,
    text_norm_bias,
    text_head,
    text_head_bias,
    log_scale,
    logit_shift,
    loss_scale,
):
    ylo_count, x_count, z_count, core_count = (lax.axis_size(a) for a in DP)
    tensor_count = lax.axis_size("tensor")
    group_count = lax.axis_size(GROUP)
    tensor_rank = lax.axis_index("tensor")
    block_rows, width = image_pooled.shape
    own_rows = block_rows // tensor_count
    pairs_total = block_rows * lax.axis_size(DP)
    slab, hidden_local = image_up.shape
    chunk = -(-hidden_local // (group_count * 4)) * 4
    hidden_mine = chunk * tensor_count

    def turned(vec):
        return (
            vec.reshape(ylo_count, x_count, z_count, core_count * slab).transpose(2, 1, 0, 3).reshape(width)
        )

    source_of = turned(jnp.arange(width, dtype=jnp.int32))
    turn = (jnp.arange(width, dtype=jnp.int32)[:, None] == source_of[None, :]).astype(low)

    def cut(arr):
        padded = jnp.pad(arr, ((0, 0), (0, chunk * group_count - hidden_local)))
        return padded.reshape(arr.shape[0], group_count, chunk)

    bias_high = image_up_bias.astype(low)
    bias_low = (image_up_bias - bias_high.astype(jnp.float32)).astype(low)
    rows = jnp.concatenate([image_up, image_down.T, bias_high[None], bias_low[None]], axis=0)
    slots = cut(rows).transpose(1, 0, 2)
    slots = jnp.broadcast_to(slots[:, None], (group_count, tensor_count) + slots.shape[1:])
    slots = slots.reshape((group_count * tensor_count,) + slots.shape[2:])
    got = lax.all_to_all(slots, GROUP + ("tensor",), 0, 0, tiled=True)
    gain_turned = turned(image_norm_gain)
    image_own = lax.dynamic_slice_in_dim(image_pooled, tensor_rank * own_rows, own_rows, 0)
    image_own = mm(image_own, turn)
    image_normed, image_inverse = norm_stats(image_own)
    ready = (image_normed * gain_turned + turned(image_norm_bias)).astype(low)
    ready_all = lax.all_gather(ready, ("ylo", "core"), axis=0, tiled=True)
    ready_all, got = lax.optimization_barrier((ready_all, got))
    ready_all = lax.all_gather(ready_all, "x", axis=0, tiled=True)

    text_float, got = lax.optimization_barrier((text_pooled, got))
    got = got.reshape(group_count, tensor_count, 2 * slab + 2, chunk)
    up_bias = (
        got[0, :, 2 * slab].astype(jnp.float32) + got[0, :, 2 * slab + 1].astype(jnp.float32)
    ).reshape(hidden_mine)
    both = got[:, :, : 2 * slab].reshape(group_count, tensor_count, 2, slab, chunk)
    both = both.transpose(0, 3, 2, 1, 4).reshape(group_count * slab, 2 * hidden_mine)
    weights = spread(both, "z").reshape(width, 2 * hidden_mine)

    text_normed, text_inverse = norm_stats(text_float.astype(jnp.float32))
    text_ready = (text_normed * text_norm_gain + text_norm_bias).astype(low)
    head_rows = text_head.shape[0]
    text_columns = lax.dynamic_slice_in_dim(text_ready, tensor_rank * head_rows, head_rows, 1)
    head_turned = mm(text_head, turn).astype(low)
    text_sent = mm(text_columns, head_turned).astype(low)
    text_total, ready_all = tensor_total(text_sent, ready_all)
    text_unit, text_invnorm = unit_rows(text_total + turned(text_head_bias))
    text_emb = text_unit.astype(low)
    ready_all, text_emb = together(ready_all, text_emb)
    up_mine = weights[:, :hidden_mine]
    down_mine = weights[:, hidden_mine:]

    hidden_pre = mm(ready_all, up_mine) + up_bias
    hidden_act, hidden_slope = gelu_parts(hidden_pre)
    image_part = mm_nt(hidden_act.astype(low), down_mine).astype(low)
    x_steps = range(1, lax.axis_size("x"))
    image_part, text_emb, text_got = together(image_part, text_emb, passed(text_emb, "x", 2))
    image_sum, text_near = together(
        sum_slots(image_part, GROUP),
        [text_emb, passed(text_emb, "x", 1), text_got, passed(text_emb, "x", 3)],
    )
    text_near = jnp.concatenate(text_near, axis=0)
    image_sum = image_sum + image_own + turned(image_down_bias)
    image_unit, image_invnorm = unit_rows(image_sum)
    image_all, text_far = together(
        spread(image_unit.astype(low), IMAGES).reshape(-1, width), passed(text_near, "core", 1)
    )

    scale_value = jnp.exp(log_scale[0])
    numbers = jnp.stack([scale_value, logit_shift[0], loss_scale[0] * scale_value / pairs_total])
    places = jnp.stack(
        [lax.axis_index(IMAGES) * own_rows, tensor_rank * own_rows, jnp.int32(own_rows)]
    ).astype(jnp.int32)
    near_coef, far_coef, image_part = pairs(numbers, places, image_all, text_near, text_far)
    far_part = mm_tn(far_coef, image_all).astype(low)
    text_part = mm_tn(near_coef, image_all) + passed(far_part, "core", 1).astype(jnp.float32)
    text_part = text_part.astype(low).reshape(-1, block_rows, width)
    image_got, text_got = together(
        swap_slots(image_part, IMAGES),
        [text_part[0]] + [passed(text_part[step], "x", -step) for step in x_steps],
    )
    text_unit_back = sum(part.astype(jnp.float32) for part in text_got).astype(low)

    image_back, slots = back_slots(image_got, image_unit, image_invnorm, group_count)
    back_all = lax.all_to_all(slots, GROUP, 0, 0, tiled=True).reshape(-1, width)
    pre_back = (mm(back_all, down_mine) * hidden_slope).astype(low)
    ready_sent = mm_nt(pre_back, up_mine).astype(low)
    ready_sent, text_got = together(ready_sent, crossed(text_unit_back, "tensor", 2))
    text_unit_back = add(text_unit_back, text_got)
    ready_back, text_got = together(
        sum_slots(ready_sent, GROUP), crossed(text_unit_back, "tensor", 1)
    )
    text_unit_back = text_unit_back.astype(jnp.float32) + text_got.astype(jnp.float32)
    image_grad = image_back + norm_backward(ready_back, image_normed, image_inverse, gain_turned)
    image_low = mm_nt(image_grad.astype(low), turn).astype(low)

    text_back = unit_backward(text_unit_back, text_unit, text_invnorm)
    head_tiles = -(-head_rows // lanes)
    head_padded = jnp.pad(head_turned, ((0, head_tiles * lanes - head_rows), (0, 0)))
    column_part = mm_nt(text_back.astype(low), head_padded).astype(low)

    tiles = width // lanes
    last = jnp.concatenate(
        [
            image_low.reshape(own_rows, tiles, lanes).transpose(1, 0, 2).reshape(-1, lanes),
            column_part.reshape(block_rows, head_tiles, lanes).transpose(1, 0, 2).reshape(-1, lanes),
        ],
        axis=0,
    )
    last = spread(last, "tensor")
    return outputs(last, text_normed, text_inverse, text_norm_gain[None])


def solution(mesh):
    grid = Mesh(mesh.devices.reshape(2, 4, 8, 2, 4), DP + ("tensor",))
    return jax.shard_map(
        per_device,
        mesh=grid,
        in_specs=(
            P(DP, None),
            P(DP, None),
            P(),
            P(),
            P(DP, "tensor"),
            P("tensor"),
            P("tensor", DP),
            P(),
            P(),
            P(),
            P("tensor", None),
            P(),
            P(),
            P(),
            P(),
        ),
        out_specs=(P(DP, None), P(DP, None)),
        check_vma=False,
    )
```

```python
import jax
import jax.numpy as jnp
from jax import lax
from jax.experimental import pallas as pl
from jax.experimental.pallas import tpu as pltpu
from jax.sharding import Mesh, PartitionSpec as P

epsilon = 1e-06
tanh_coef = 0.7978845608028654
cubic_coef = 0.044715
low = jnp.bfloat16
lanes = 128
DP = ("ylo", "x", "z", "core")
GROUP = ("x", "ylo", "core")
IMAGES = ("z", "ylo")


def gelu_parts(preact):
    inside = tanh_coef * (preact + cubic_coef * preact * preact * preact)
    tangent = jnp.tanh(inside)
    activated = 0.5 * preact * (1.0 + tangent)
    derivative = 0.5 * (1.0 + tangent) + 0.5 * preact * (1.0 - tangent * tangent) * tanh_coef * (
        1.0 + 3.0 * cubic_coef * preact * preact
    )
    return (activated, derivative)


def norm_stats(source):
    centre = source - jnp.mean(source, axis=1, keepdims=True)
    inverse = lax.rsqrt(jnp.mean(centre * centre, axis=1, keepdims=True) + epsilon)
    return (centre * inverse, inverse)


def norm_backward(upstream, normed, inverse, gain_vec):
    scaled = upstream * gain_vec
    return inverse * (
        scaled
        - jnp.mean(scaled, axis=1, keepdims=True)
        - normed * jnp.mean(scaled * normed, axis=1, keepdims=True)
    )


def unit_rows(total):
    inverse = lax.rsqrt(jnp.sum(total * total, axis=1, keepdims=True) + epsilon)
    return (total * inverse, inverse)


def unit_backward(upstream, unit, inverse):
    return (upstream - unit * jnp.sum(unit * upstream, axis=1, keepdims=True)) * inverse


def mm(a, b):
    return jnp.dot(a, b, preferred_element_type=jnp.float32)


def mm_nt(a, b):
    return lax.dot_general(a, b, (((1,), (1,)), ((), ())), preferred_element_type=jnp.float32)


def mm_tn(a, b):
    return lax.dot_general(a, b, (((0,), (0,)), ((), ())), preferred_element_type=jnp.float32)


def spread(block, axes):
    count = lax.axis_size(axes)
    slots = jnp.broadcast_to(block[None], (count,) + block.shape)
    return lax.all_to_all(slots, axes, 0, 0, tiled=True)


def swap_slots(partial, axes):
    count = lax.axis_size(axes)
    slots = partial.astype(low).reshape(count, partial.shape[0] // count, partial.shape[1])
    return lax.all_to_all(slots, axes, 0, 0, tiled=True)


def sum_slots(partial, axes):
    return jnp.sum(swap_slots(partial, axes).astype(jnp.float32), axis=0)


def passed(block, axis, step):
    count = lax.axis_size(axis)
    return lax.ppermute(block, axis, [(i, (i + step) % count) for i in range(count)])


def crossed(block, axis, bits):
    return lax.ppermute(block, axis, [(i, i ^ bits) for i in range(lax.axis_size(axis))])


def add(one, other):
    return (one.astype(jnp.float32) + other.astype(jnp.float32)).astype(low)


def together(*values):
    return lax.optimization_barrier(values)


def tensor_total(sent, earlier):
    got = [passed(sent, "tensor", step) for step in range(1, lax.axis_size("tensor"))]
    got, earlier = lax.optimization_barrier((got, earlier))
    total = sent.astype(jnp.float32)
    for part in got:
        total = total + part.astype(jnp.float32)
    return (total, earlier)


def pair_kernel(number_ref, place_ref, image_ref, near_ref, far_ref, near_coef_ref, far_coef_ref, part_ref):
    scale_value, shift, factor = (number_ref[i] for i in range(3))
    image = image_ref[...]
    near = near_ref[...]
    far = far_ref[...]
    chance = jax.nn.sigmoid(scale_value * mm_nt(image, near) + shift)
    image_at = lax.broadcasted_iota(jnp.int32, chance.shape, 0) - place_ref[0]
    text_at = lax.broadcasted_iota(jnp.int32, chance.shape, 1) - place_ref[1]
    same = (image_at == text_at) & (image_at >= 0) & (image_at < place_ref[2])
    near_coef = (factor * (chance - same.astype(jnp.float32))).astype(low)
    far_coef = (factor * jax.nn.sigmoid(scale_value * mm_nt(image, far) + shift)).astype(low)
    near_coef_ref[...] = near_coef
    far_coef_ref[...] = far_coef
    part_ref[...] = (mm(near_coef, near) + mm(far_coef, far)).astype(low)


def back_kernel(got_ref, unit_ref, inverse_ref, back_ref, slots_ref):
    upstream = jnp.sum(got_ref[...].astype(jnp.float32), axis=0)
    back = unit_backward(upstream, unit_ref[...], inverse_ref[...])
    back_ref[...] = back
    sent = back.astype(low)
    for slot in range(slots_ref.shape[0]):
        slots_ref[slot] = sent


def back_slots(got, unit, inverse, count):
    vmem = pl.BlockSpec(memory_space=pltpu.VMEM)
    return pl.pallas_call(
        back_kernel,
        out_shape=(
            jax.ShapeDtypeStruct(unit.shape, jnp.float32),
            jax.ShapeDtypeStruct((count,) + unit.shape, low),
        ),
        in_specs=[vmem, vmem, vmem],
        out_specs=(vmem, vmem),
        compiler_params=pltpu.CompilerParams(vmem_limit_bytes=10 * 1024 * 1024),
    )(got, unit, inverse)


def output_kernel(last_ref, normed_ref, inverse_ref, gain_ref, image_ref, text_ref):
    count = last_ref.shape[0]
    rows, width = image_ref.shape
    own, tiles = rows // count, width // lanes
    for slot in range(count):
        for tile in range(tiles):
            image_ref[slot * own : (slot + 1) * own, tile * lanes : (tile + 1) * lanes] = last_ref[
                slot, tile * own : (tile + 1) * own
            ].astype(jnp.float32)
    pieces = []
    for slot in range(count):
        left = width // count
        for at in range(tiles * own, last_ref.shape[1], rows):
            piece = last_ref[slot, at : at + rows].astype(jnp.float32)
            pieces.append(piece[:, : min(left, lanes)])
            left -= lanes
    column_back = jnp.concatenate(pieces, axis=1)
    text_ref[...] = norm_backward(column_back, normed_ref[...], inverse_ref[...], gain_ref[...])


def outputs(last, normed, inverse, gain):
    vmem = pl.BlockSpec(memory_space=pltpu.VMEM)
    return pl.pallas_call(
        output_kernel,
        out_shape=(jax.ShapeDtypeStruct(normed.shape, jnp.float32),) * 2,
        in_specs=[vmem] * 4,
        out_specs=(vmem, vmem),
        compiler_params=pltpu.CompilerParams(vmem_limit_bytes=10 * 1024 * 1024),
    )(last, normed, inverse, gain)


def pairs(numbers, places, image, near, far):
    rows, width = image.shape
    vmem, smem = pl.BlockSpec(memory_space=pltpu.VMEM), pl.BlockSpec(memory_space=pltpu.SMEM)
    return pl.pallas_call(
        pair_kernel,
        out_shape=(
            jax.ShapeDtypeStruct((rows, near.shape[0]), low),
            jax.ShapeDtypeStruct((rows, far.shape[0]), low),
            jax.ShapeDtypeStruct((rows, width), low),
        ),
        in_specs=[smem, smem, vmem, vmem, vmem],
        out_specs=(vmem, vmem, vmem),
        compiler_params=pltpu.CompilerParams(vmem_limit_bytes=10 * 1024 * 1024),
    )(numbers, places, image, near, far)


def per_device(
    image_pooled,
    text_pooled,
    image_norm_gain,
    image_norm_bias,
    image_up,
    image_up_bias,
    image_down,
    image_down_bias,
    text_norm_gain,
    text_norm_bias,
    text_head,
    text_head_bias,
    log_scale,
    logit_shift,
    loss_scale,
):
    ylo_count, x_count, z_count, core_count = (lax.axis_size(a) for a in DP)
    tensor_count = lax.axis_size("tensor")
    group_count = lax.axis_size(GROUP)
    tensor_rank = lax.axis_index("tensor")
    block_rows, width = image_pooled.shape
    own_rows = block_rows // tensor_count
    pairs_total = block_rows * lax.axis_size(DP)
    slab, hidden_local = image_up.shape
    chunk = -(-hidden_local // (group_count * 4)) * 4
    hidden_mine = chunk * tensor_count

    def turned(vec):
        return (
            vec.reshape(ylo_count, x_count, z_count, core_count * slab).transpose(2, 1, 0, 3).reshape(width)
        )

    source_of = turned(jnp.arange(width, dtype=jnp.int32))
    turn = (jnp.arange(width, dtype=jnp.int32)[:, None] == source_of[None, :]).astype(low)

    def cut(arr):
        padded = jnp.pad(arr, ((0, 0), (0, chunk * group_count - hidden_local)))
        return padded.reshape(arr.shape[0], group_count, chunk)

    bias_row = image_up_bias[None]
    bias_high = bias_row.astype(low)
    bias_low = (bias_row - bias_high.astype(jnp.float32)).astype(low)
    rows = jnp.concatenate([image_up, image_down.T, bias_high, bias_low], axis=0)
    slots = cut(rows).transpose(1, 0, 2)
    slots = jnp.broadcast_to(slots[:, None], (group_count, tensor_count) + slots.shape[1:])
    slots = slots.reshape((group_count * tensor_count,) + slots.shape[2:])
    got = lax.all_to_all(slots, GROUP + ("tensor",), 0, 0, tiled=True)
    gain_turned = turned(image_norm_gain)
    image_own = lax.dynamic_slice_in_dim(image_pooled, tensor_rank * own_rows, own_rows, 0)
    image_own = mm(image_own, turn)
    image_normed, image_inverse = norm_stats(image_own)
    ready = (image_normed * gain_turned + turned(image_norm_bias)).astype(low)
    ready_all = lax.all_gather(ready, ("ylo", "core"), axis=0, tiled=True)
    ready_all, got = lax.optimization_barrier((ready_all, got))
    ready_all = lax.all_gather(ready_all, "x", axis=0, tiled=True)

    text_float, got = lax.optimization_barrier((text_pooled, got))
    got = got.reshape(group_count, tensor_count, 2 * slab + 2, chunk)
    up_bias = (
        got[0, :, 2 * slab].astype(jnp.float32) + got[0, :, 2 * slab + 1].astype(jnp.float32)
    ).reshape(hidden_mine)
    both = got[:, :, : 2 * slab].reshape(group_count, tensor_count, 2, slab, chunk)
    both = both.transpose(0, 3, 2, 1, 4).reshape(group_count * slab, 2 * hidden_mine)
    weights = spread(both, "z").reshape(width, 2 * hidden_mine)

    text_normed, text_inverse = norm_stats(text_float.astype(jnp.float32))
    text_ready = (text_normed * text_norm_gain + text_norm_bias).astype(low)
    head_rows = text_head.shape[0]
    text_columns = lax.dynamic_slice_in_dim(text_ready, tensor_rank * head_rows, head_rows, 1)
    head_turned = mm(text_head, turn).astype(low)
    text_sent = mm(text_columns, head_turned).astype(low)
    text_total, ready_all = tensor_total(text_sent, ready_all)
    text_unit, text_invnorm = unit_rows(text_total + turned(text_head_bias))
    text_emb = text_unit.astype(low)
    ready_all, text_emb = together(ready_all, text_emb)
    up_mine = weights[:, :hidden_mine]
    down_mine = weights[:, hidden_mine:]

    hidden_pre = mm(ready_all, up_mine) + up_bias
    hidden_act, hidden_slope = gelu_parts(hidden_pre)
    image_part = mm_nt(hidden_act.astype(low), down_mine).astype(low)
    x_steps = range(1, lax.axis_size("x"))
    image_part, text_near = together(
        image_part, [text_emb] + [passed(text_emb, "x", step) for step in (2, 1, 3)]
    )
    text_near = [text_near[0], text_near[2], text_near[1], text_near[3]]
    image_sum = sum_slots(image_part, GROUP)
    text_near = jnp.concatenate(text_near, axis=0)
    image_sum = image_sum + image_own + turned(image_down_bias)
    image_unit, image_invnorm = unit_rows(image_sum)
    image_all, text_far = together(
        spread(image_unit.astype(low), IMAGES).reshape(-1, width), passed(text_near, "core", 1)
    )

    scale_value = jnp.exp(log_scale[0])
    numbers = jnp.stack([scale_value, logit_shift[0], loss_scale[0] * scale_value / pairs_total])
    places = jnp.stack(
        [lax.axis_index(IMAGES) * own_rows, tensor_rank * own_rows, jnp.int32(own_rows)]
    ).astype(jnp.int32)
    near_coef, far_coef, image_part = pairs(numbers, places, image_all, text_near, text_far)
    far_part = mm_tn(far_coef, image_all).astype(low)
    text_part = mm_tn(near_coef, image_all) + passed(far_part, "core", 1).astype(jnp.float32)
    text_part = text_part.astype(low).reshape(-1, block_rows, width)
    image_got, text_got = together(
        swap_slots(image_part, IMAGES),
        [text_part[0]] + [passed(text_part[step], "x", -step) for step in x_steps],
    )
    text_unit_back = sum(part.astype(jnp.float32) for part in text_got).astype(low)

    image_back, slots = back_slots(image_got, image_unit, image_invnorm, group_count)
    back_all = lax.all_to_all(slots, GROUP, 0, 0, tiled=True).reshape(-1, width)
    pre_back = (mm(back_all, down_mine) * hidden_slope).astype(low)
    ready_sent = mm_nt(pre_back, up_mine).astype(low)
    ready_sent, text_got = together(ready_sent, crossed(text_unit_back, "tensor", 2))
    text_unit_back = add(text_unit_back, text_got)
    ready_back, text_got = together(
        sum_slots(ready_sent, GROUP), crossed(text_unit_back, "tensor", 1)
    )
    text_unit_back = text_unit_back.astype(jnp.float32) + text_got.astype(jnp.float32)
    image_grad = image_back + norm_backward(ready_back, image_normed, image_inverse, gain_turned)
    image_low = mm_nt(image_grad.astype(low), turn).astype(low)

    text_back = unit_backward(text_unit_back, text_unit, text_invnorm)
    head_tiles = -(-head_rows // lanes)
    head_padded = jnp.pad(head_turned, ((0, head_tiles * lanes - head_rows), (0, 0)))
    column_part = mm_nt(text_back.astype(low), head_padded).astype(low)

    tiles = width // lanes
    last = jnp.concatenate(
        [
            image_low.reshape(own_rows, tiles, lanes).transpose(1, 0, 2).reshape(-1, lanes),
            column_part.reshape(block_rows, head_tiles, lanes).transpose(1, 0, 2).reshape(-1, lanes),
        ],
        axis=0,
    )
    last = spread(last, "tensor")
    return outputs(last, text_normed, text_inverse, text_norm_gain[None])


def solution(mesh):
    grid = Mesh(mesh.devices.reshape(2, 4, 8, 2, 4), DP + ("tensor",))
    return jax.shard_map(
        per_device,
        mesh=grid,
        in_specs=(
            P(DP, None),
            P(DP, None),
            P(),
            P(),
            P(DP, "tensor"),
            P("tensor"),
            P("tensor", DP),
            P(),
            P(),
            P(),
            P("tensor", None),
            P(),
            P(),
            P(),
            P(),
        ),
        out_specs=(P(DP, None), P(DP, None)),
        check_vma=False,
    )
```

```python
import jax
import jax.numpy as jnp
from jax import lax
from jax.experimental import pallas as pl
from jax.experimental.pallas import tpu as pltpu
from jax.sharding import Mesh, PartitionSpec as P

epsilon = 1e-06
tanh_coef = 0.7978845608028654
cubic_coef = 0.044715
low = jnp.bfloat16
lanes = 128
DP = ("ylo", "x", "z", "core")
GROUP = ("x", "ylo", "core")
IMAGES = ("z", "ylo")


def gelu_parts(preact):
    inside = tanh_coef * (preact + cubic_coef * preact * preact * preact)
    tangent = jnp.tanh(inside)
    activated = 0.5 * preact * (1.0 + tangent)
    derivative = 0.5 * (1.0 + tangent) + 0.5 * preact * (1.0 - tangent * tangent) * tanh_coef * (
        1.0 + 3.0 * cubic_coef * preact * preact
    )
    return (activated, derivative)


def norm_stats(source):
    centre = source - jnp.mean(source, axis=1, keepdims=True)
    inverse = lax.rsqrt(jnp.mean(centre * centre, axis=1, keepdims=True) + epsilon)
    return (centre * inverse, inverse)


def norm_backward(upstream, normed, inverse, gain_vec):
    scaled = upstream * gain_vec
    return inverse * (
        scaled
        - jnp.mean(scaled, axis=1, keepdims=True)
        - normed * jnp.mean(scaled * normed, axis=1, keepdims=True)
    )


def unit_rows(total):
    inverse = lax.rsqrt(jnp.sum(total * total, axis=1, keepdims=True) + epsilon)
    return (total * inverse, inverse)


def unit_backward(upstream, unit, inverse):
    return (upstream - unit * jnp.sum(unit * upstream, axis=1, keepdims=True)) * inverse


def mm(a, b):
    return jnp.dot(a, b, preferred_element_type=jnp.float32)


def mm_nt(a, b):
    return lax.dot_general(a, b, (((1,), (1,)), ((), ())), preferred_element_type=jnp.float32)


def mm_tn(a, b):
    return lax.dot_general(a, b, (((0,), (0,)), ((), ())), preferred_element_type=jnp.float32)


def spread(block, axes):
    count = lax.axis_size(axes)
    slots = jnp.broadcast_to(block[None], (count,) + block.shape)
    return lax.all_to_all(slots, axes, 0, 0, tiled=True)


def swap_slots(partial, axes):
    count = lax.axis_size(axes)
    slots = partial.astype(low).reshape(count, partial.shape[0] // count, partial.shape[1])
    return lax.all_to_all(slots, axes, 0, 0, tiled=True)


def sum_slots(partial, axes):
    return jnp.sum(swap_slots(partial, axes).astype(jnp.float32), axis=0)


def passed(block, axis, step):
    count = lax.axis_size(axis)
    return lax.ppermute(block, axis, [(i, (i + step) % count) for i in range(count)])


def crossed(block, axis, bits):
    return lax.ppermute(block, axis, [(i, i ^ bits) for i in range(lax.axis_size(axis))])


def add(one, other):
    return (one.astype(jnp.float32) + other.astype(jnp.float32)).astype(low)


def together(*values):
    return lax.optimization_barrier(values)


def tensor_total(sent, earlier):
    got = [passed(sent, "tensor", step) for step in range(1, lax.axis_size("tensor"))]
    got, earlier = lax.optimization_barrier((got, earlier))
    total = sent.astype(jnp.float32)
    for part in got:
        total = total + part.astype(jnp.float32)
    return (total, earlier)


def pair_kernel(number_ref, place_ref, image_ref, near_ref, far_ref, near_coef_ref, far_coef_ref, part_ref):
    scale_value, shift, factor = (number_ref[i] for i in range(3))
    image = image_ref[...]
    near = near_ref[...]
    far = far_ref[...]
    chance = jax.nn.sigmoid(scale_value * mm_nt(image, near) + shift)
    image_at = lax.broadcasted_iota(jnp.int32, chance.shape, 0) - place_ref[0]
    text_at = lax.broadcasted_iota(jnp.int32, chance.shape, 1) - place_ref[1]
    same = (image_at == text_at) & (image_at >= 0) & (image_at < place_ref[2])
    near_coef = (factor * (chance - same.astype(jnp.float32))).astype(low)
    far_coef = (factor * jax.nn.sigmoid(scale_value * mm_nt(image, far) + shift)).astype(low)
    near_coef_ref[...] = near_coef
    far_coef_ref[...] = far_coef
    part_ref[...] = (mm(near_coef, near) + mm(far_coef, far)).astype(low)


def back_kernel(got_ref, unit_ref, inverse_ref, back_ref, slots_ref):
    upstream = jnp.sum(got_ref[...].astype(jnp.float32), axis=0)
    back = unit_backward(upstream, unit_ref[...], inverse_ref[...])
    back_ref[...] = back
    sent = back.astype(low)
    for slot in range(slots_ref.shape[0]):
        slots_ref[slot] = sent


def back_slots(got, unit, inverse, count):
    vmem = pl.BlockSpec(memory_space=pltpu.VMEM)
    return pl.pallas_call(
        back_kernel,
        out_shape=(
            jax.ShapeDtypeStruct(unit.shape, jnp.float32),
            jax.ShapeDtypeStruct((count,) + unit.shape, low),
        ),
        in_specs=[vmem, vmem, vmem],
        out_specs=(vmem, vmem),
        compiler_params=pltpu.CompilerParams(vmem_limit_bytes=10 * 1024 * 1024),
    )(got, unit, inverse)


def output_kernel(last_ref, normed_ref, inverse_ref, gain_ref, image_ref, text_ref):
    count = last_ref.shape[0]
    rows, width = image_ref.shape
    own, tiles = rows // count, width // lanes
    for slot in range(count):
        for tile in range(tiles):
            image_ref[slot * own : (slot + 1) * own, tile * lanes : (tile + 1) * lanes] = last_ref[
                slot, tile * own : (tile + 1) * own
            ].astype(jnp.float32)
    pieces = []
    for slot in range(count):
        left = width // count
        for at in range(tiles * own, last_ref.shape[1], rows):
            piece = last_ref[slot, at : at + rows].astype(jnp.float32)
            pieces.append(piece[:, : min(left, lanes)])
            left -= lanes
    column_back = jnp.concatenate(pieces, axis=1)
    text_ref[...] = norm_backward(column_back, normed_ref[...], inverse_ref[...], gain_ref[...])


def outputs(last, normed, inverse, gain):
    vmem = pl.BlockSpec(memory_space=pltpu.VMEM)
    return pl.pallas_call(
        output_kernel,
        out_shape=(jax.ShapeDtypeStruct(normed.shape, jnp.float32),) * 2,
        in_specs=[vmem] * 4,
        out_specs=(vmem, vmem),
        compiler_params=pltpu.CompilerParams(vmem_limit_bytes=10 * 1024 * 1024),
    )(last, normed, inverse, gain)


def pairs(numbers, places, image, near, far):
    rows, width = image.shape
    vmem, smem = pl.BlockSpec(memory_space=pltpu.VMEM), pl.BlockSpec(memory_space=pltpu.SMEM)
    return pl.pallas_call(
        pair_kernel,
        out_shape=(
            jax.ShapeDtypeStruct((rows, near.shape[0]), low),
            jax.ShapeDtypeStruct((rows, far.shape[0]), low),
            jax.ShapeDtypeStruct((rows, width), low),
        ),
        in_specs=[smem, smem, vmem, vmem, vmem],
        out_specs=(vmem, vmem, vmem),
        compiler_params=pltpu.CompilerParams(vmem_limit_bytes=10 * 1024 * 1024),
    )(numbers, places, image, near, far)


def per_device(
    image_pooled,
    text_pooled,
    image_norm_gain,
    image_norm_bias,
    image_up,
    image_up_bias,
    image_down,
    image_down_bias,
    text_norm_gain,
    text_norm_bias,
    text_head,
    text_head_bias,
    log_scale,
    logit_shift,
    loss_scale,
):
    ylo_count, x_count, z_count, core_count = (lax.axis_size(a) for a in DP)
    tensor_count = lax.axis_size("tensor")
    group_count = lax.axis_size(GROUP)
    tensor_rank = lax.axis_index("tensor")
    block_rows, width = image_pooled.shape
    own_rows = block_rows // tensor_count
    pairs_total = block_rows * lax.axis_size(DP)
    slab, hidden_local = image_up.shape
    chunk = -(-hidden_local // (group_count * 4)) * 4
    hidden_mine = chunk * tensor_count

    def turned(vec):
        return (
            vec.reshape(ylo_count, x_count, z_count, core_count * slab).transpose(2, 1, 0, 3).reshape(width)
        )

    source_of = turned(jnp.arange(width, dtype=jnp.int32))
    turn = (jnp.arange(width, dtype=jnp.int32)[:, None] == source_of[None, :]).astype(low)

    def cut(arr):
        padded = jnp.pad(arr, ((0, 0), (0, chunk * group_count - hidden_local)))
        return padded.reshape(arr.shape[0], group_count, chunk)

    bias_row = image_up_bias[None]
    bias_high = bias_row.astype(low)
    bias_low = (bias_row - bias_high.astype(jnp.float32)).astype(low)
    rows = jnp.concatenate([image_up, image_down.T, bias_high, bias_low], axis=0)
    slots = cut(rows).transpose(1, 0, 2)
    slots = jnp.broadcast_to(slots[:, None], (group_count, tensor_count) + slots.shape[1:])
    slots = slots.reshape((group_count * tensor_count,) + slots.shape[2:])
    got = lax.all_to_all(slots, GROUP + ("tensor",), 0, 0, tiled=True)
    gain_turned = turned(image_norm_gain)
    image_own = lax.dynamic_slice_in_dim(image_pooled, tensor_rank * own_rows, own_rows, 0)
    image_own = mm(image_own, turn)
    image_normed, image_inverse = norm_stats(image_own)
    ready = (image_normed * gain_turned + turned(image_norm_bias)).astype(low)
    ready_all = lax.all_gather(ready, ("ylo", "core"), axis=0, tiled=True)
    ready_all, got = lax.optimization_barrier((ready_all, got))
    ready_all = lax.all_gather(ready_all, "x", axis=0, tiled=True)

    text_float, got = lax.optimization_barrier((text_pooled, got))
    got = got.reshape(group_count, tensor_count, 2 * slab + 2, chunk)
    up_bias = (
        got[0, :, 2 * slab].astype(jnp.float32) + got[0, :, 2 * slab + 1].astype(jnp.float32)
    ).reshape(hidden_mine)
    both = got[:, :, : 2 * slab].reshape(group_count, tensor_count, 2, slab, chunk)
    both = both.transpose(0, 3, 2, 1, 4).reshape(group_count * slab, 2 * hidden_mine)
    weights = spread(both, "z").reshape(width, 2 * hidden_mine)

    text_normed, text_inverse = norm_stats(text_float.astype(jnp.float32))
    text_ready = (text_normed * text_norm_gain + text_norm_bias).astype(low)
    head_rows = text_head.shape[0]
    text_columns = lax.dynamic_slice_in_dim(text_ready, tensor_rank * head_rows, head_rows, 1)
    head_turned = mm(text_head, turn).astype(low)
    text_sent = mm(text_columns, head_turned).astype(low)
    text_total, ready_all = tensor_total(text_sent, ready_all)
    text_unit, text_invnorm = unit_rows(text_total + turned(text_head_bias))
    text_emb = text_unit.astype(low)
    ready_all, text_emb = together(ready_all, text_emb)
    up_mine = weights[:, :hidden_mine]
    down_mine = weights[:, hidden_mine:]

    hidden_pre = mm(ready_all, up_mine) + up_bias
    hidden_act = gelu_parts(hidden_pre)[0]
    image_part = mm_nt(hidden_act.astype(low), down_mine).astype(low)
    x_steps = range(1, lax.axis_size("x"))
    image_part, text_near = together(
        image_part, [text_emb] + [passed(text_emb, "x", step) for step in (2, 1, 3)]
    )
    text_near = [text_near[0], text_near[2], text_near[1], text_near[3]]
    image_sum, hidden_pre = together(sum_slots(image_part, GROUP), hidden_pre)
    text_near = jnp.concatenate(text_near, axis=0)
    image_sum = image_sum + image_own + turned(image_down_bias)
    image_unit, image_invnorm = unit_rows(image_sum)
    image_all, text_far, hidden_slope = together(
        spread(image_unit.astype(low), IMAGES).reshape(-1, width),
        passed(text_near, "core", 1),
        gelu_parts(hidden_pre)[1],
    )

    scale_value = jnp.exp(log_scale[0])
    numbers = jnp.stack([scale_value, logit_shift[0], loss_scale[0] * scale_value / pairs_total])
    places = jnp.stack(
        [lax.axis_index(IMAGES) * own_rows, tensor_rank * own_rows, jnp.int32(own_rows)]
    ).astype(jnp.int32)
    near_coef, far_coef, image_part = pairs(numbers, places, image_all, text_near, text_far)
    far_part = mm_tn(far_coef, image_all).astype(low)
    text_part = mm_tn(near_coef, image_all) + passed(far_part, "core", 1).astype(jnp.float32)
    text_part = text_part.astype(low).reshape(-1, block_rows, width)
    image_got, text_got = together(
        swap_slots(image_part, IMAGES),
        [text_part[0]] + [passed(text_part[step], "x", -step) for step in x_steps],
    )
    text_unit_back = sum(part.astype(jnp.float32) for part in text_got).astype(low)

    image_back, slots = back_slots(image_got, image_unit, image_invnorm, group_count)
    back_all = lax.all_to_all(slots, GROUP, 0, 0, tiled=True).reshape(-1, width)
    pre_back = (mm(back_all, down_mine) * hidden_slope).astype(low)
    ready_sent = mm_nt(pre_back, up_mine).astype(low)
    ready_sent, text_got = together(ready_sent, crossed(text_unit_back, "tensor", 2))
    text_unit_back = add(text_unit_back, text_got)
    ready_back, text_got = together(
        sum_slots(ready_sent, GROUP), crossed(text_unit_back, "tensor", 1)
    )
    text_unit_back = text_unit_back.astype(jnp.float32) + text_got.astype(jnp.float32)
    image_grad = image_back + norm_backward(ready_back, image_normed, image_inverse, gain_turned)
    image_low = mm_nt(image_grad.astype(low), turn).astype(low)

    text_back = unit_backward(text_unit_back, text_unit, text_invnorm)
    head_tiles = -(-head_rows // lanes)
    head_padded = jnp.pad(head_turned, ((0, head_tiles * lanes - head_rows), (0, 0)))
    column_part = mm_nt(text_back.astype(low), head_padded).astype(low)

    tiles = width // lanes
    last = jnp.concatenate(
        [
            image_low.reshape(own_rows, tiles, lanes).transpose(1, 0, 2).reshape(-1, lanes),
            column_part.reshape(block_rows, head_tiles, lanes).transpose(1, 0, 2).reshape(-1, lanes),
        ],
        axis=0,
    )
    last = spread(last, "tensor")
    return outputs(last, text_normed, text_inverse, text_norm_gain[None])


def solution(mesh):
    grid = Mesh(mesh.devices.reshape(2, 4, 8, 2, 4), DP + ("tensor",))
    return jax.shard_map(
        per_device,
        mesh=grid,
        in_specs=(
            P(DP, None),
            P(DP, None),
            P(),
            P(),
            P(DP, "tensor"),
            P("tensor"),
            P("tensor", DP),
            P(),
            P(),
            P(),
            P("tensor", None),
            P(),
            P(),
            P(),
            P(),
        ),
        out_specs=(P(DP, None), P(DP, None)),
        check_vma=False,
    )
```
